32 devices in a mesh: groups: 2 (over x), sector: 8 (over z, y), op: 2 (over core).
Axes of the slice: x: 2, y: 2, z: 4, core: 2. Of those that a mesh axis runs over, the one named last changes fastest.
Arguments:
- wavefunction: bfloat16 [48, 256, 256], P(('groups', 'sector')), parts along dimension 0, may hold values from -18 to 18
- left_ops: bfloat16 [32, 48, 256, 256], P('op', ('groups', 'sector')), parts along dimension 1, may hold values from -0.375 to 0.375
- right_ops: bfloat16 [32, 48, 256, 256], P('op', ('groups', 'sector')), parts along dimension 1, may hold values from -0.125 to 0.125
- energy: float32 [48], P(('groups', 'sector')), parts along dimension 0, may hold values from 0.5 to 4
- term_class: int32 [32], P('op'), may hold values from 0 to 4
- target_sector: int32 [48, 5], P('groups'), parts along dimension 0, may hold values from 0 to 23, as said below
Outputs:
- sigma: bfloat16 [48, 256, 256], P(('groups', 'sector'), 'op'), parts along dimension 0
- residual: bfloat16 [48, 256, 256], P(('groups', 'sector'), 'op'), parts along dimension 0
The draws below stay inside these ranges and needn't reach their ends.
There are 2 independent parts, one for each index of `groups`. The reference program is written for one: setup_inputs(seed, part) draws one part's arguments, and reference() takes and returns one part's arrays. A program takes and returns all parts, laid end to end along the dimension named above; an argument that names none is the same for every part. Nothing has to cross between parts.
Inputs may be any that keep to these rules, and one draw needn't show every extreme that they name: target_sector[s, c] is a sector of the index (s // 3 + o) mod 8 of sector, with o = 0, 1, -1, 2, -2 for c = 0, 1, 2, 3, 4; target_sector[s, 0] = s.
All inputs are finite; a program needn't handle non-finite values.
Results may differ from the reference program's by a relative error of at most 0.0045.
Values sent between devices are 32-bit elements; how exact they have to be, the bound alone decides.
A program may use at most 128 MiB of HBM per device.

```python
import math
import jax
import jax.numpy as jnp
from jax import lax

BLOCK = 256
TERMS = 32
CLASSES = 5
SEC_DEV = 3
SECTORS = 24


def draw_wavefunction(key, part):
    key = jax.random.fold_in(key, 3)
    first, second = jax.random.split(key)
    ramp = jnp.exp(jnp.log(3.0) * jnp.arange(SECTORS, dtype=jnp.float32) / (SECTORS - 1))
    base = jnp.clip(jax.random.normal(first, (SECTORS, BLOCK, BLOCK), jnp.float32), -4.0, 4.0)
    scales = jax.random.uniform(second, (SECTORS, BLOCK, 1), jnp.float32, 0.5, 1.5)
    return (base * scales * ramp[:, None, None]).astype(jnp.bfloat16)


def draw_target_sector(key, part):
    key = jax.random.fold_in(key, 7)
    owners = jnp.arange(SECTORS, dtype=jnp.int32) // SEC_DEV
    cycle_size = SECTORS // SEC_DEV
    offsets = jnp.array([0, 1, -1, 2, -2], dtype=jnp.int32)
    slot_ids = jax.random.randint(key, (SECTORS, CLASSES), 0, SEC_DEV, dtype=jnp.int32)
    devices = (owners[:, None] + offsets[None, :]) % cycle_size
    chosen = devices * SEC_DEV + slot_ids
    return chosen.at[:, 0].set(jnp.arange(SECTORS, dtype=jnp.int32))


def with_ends(entries, stream_key, smallest, largest):
    longest = entries.shape.index(max(entries.shape))
    spots = []
    for shift in (0, 1):
        where = [jax.random.randint(jax.random.fold_in(stream_key, axis), (), 0, length) for axis, length in enumerate(entries.shape)]
        where[longest] = (where[longest] + shift) % entries.shape[longest]
        spots.append(tuple(where))
    return entries.at[spots[0]].set(smallest).at[spots[1]].set(largest)


def levels(stream_key, extent, shards, low, largest):
    def one(position, parts):
        heights = jax.random.uniform(jax.random.fold_in(jax.random.fold_in(stream_key, 6), position), (parts,), jnp.float32, low / len(shards), largest / len(shards))
        return jnp.repeat(jnp.exp(heights), extent[position] // parts).reshape((-1,) + (1,) * (len(extent) - position - 1))

    loudness = one(*shards[0])
    for cut in shards[1:]:
        loudness = loudness * one(*cut)
    return loudness


def scatter_about(own_key, shape, deviation, reach, cuts=(), kind=jnp.bfloat16):
    drawn = jax.random.normal(own_key, shape, jnp.float32) * deviation
    if len(cuts) > 0:
        drawn = levels(own_key, shape, cuts, -0.22, 0.18) * drawn
    return jnp.clip(drawn, min=-reach, max=reach).astype(kind)


def setup_inputs(seed: int = 0, part: int = 0) -> dict:
    arg_keys = jax.random.split(jax.random.key(seed), 7)
    part_splits = jax.random.split(jax.random.fold_in(arg_keys[6], part), 7)
    return {
        "wavefunction": draw_wavefunction(jax.random.fold_in(jax.random.fold_in(arg_keys[6], part), 71), part),
        "left_ops": scatter_about(part_splits[1], (TERMS, SECTORS, BLOCK, BLOCK), BLOCK ** -0.5, 0.375, ((0, 2), (1, 8))),
        "right_ops": scatter_about(part_splits[2], (TERMS, SECTORS, BLOCK, BLOCK), (BLOCK * TERMS // 4) ** -0.5, 0.125, ((0, 2), (1, 8))),
        "energy": jnp.clip(jnp.exp(math.log(4.0) - 2.0794415 * jax.random.uniform(part_splits[3], (SECTORS,), jnp.float32) ** levels(part_splits[3], (SECTORS,), ((0, 8),), -0.2, 0.2)), 0.5, 4.0),
        "term_class": with_ends(jax.random.randint(arg_keys[4], (TERMS,), 0, CLASSES), jax.random.fold_in(arg_keys[4], 1), 0, CLASSES - 1).astype(jnp.int32),
        "target_sector": draw_target_sector(jax.random.fold_in(jax.random.fold_in(arg_keys[6], part), 71), part),
    }


def reference(wavefunction, left_ops, right_ops, energy, term_class, target_sector):
    amplitude = wavefunction.astype(jnp.float32)

    def one_term(accrued, inputs):
        left_block, right_block, class_id = inputs
        halves = jnp.einsum("sij,sjl->sil", left_block.astype(jnp.float32), amplitude).astype(jnp.bfloat16)
        product = jnp.einsum("sil,sml->sim", halves.astype(jnp.float32), right_block.astype(jnp.float32))
        targets = lax.dynamic_index_in_dim(target_sector, class_id, 1, keepdims=False).astype(jnp.int32)
        return accrued.at[targets].add(product), None

    starting = energy[:, None, None] * amplitude
    sigma_full, unused = lax.scan(one_term, starting, (left_ops, right_ops, term_class))
    quotient = jnp.sum(amplitude * sigma_full) / jnp.sum(amplitude * amplitude)
    return sigma_full.astype(jnp.bfloat16), (sigma_full - quotient * amplitude).astype(jnp.bfloat16)
```

```python
import functools

import jax
import jax.numpy as jnp
from jax import lax
from jax.experimental import pallas as pl
from jax.experimental.pallas import tpu as pltpu
from jax.sharding import PartitionSpec as P

MESH = pl.DeviceIdType.MESH
GROUP = 4
OWN, TO_PEER, VIA_PEER, JOINED, ALONE = range(5)


def kernel(n, n_op, tc, ts, energy, w_ref, left, right, sigma_out, resid_out,
           lbuf, rbuf, acc, sib, tot, peer_in, via_in, alone_in, joined_in, joined, sig, scal,
           lsem, rsem, sib_s, sib_r, peer_s, peer_r, via_s, via_r, alone_s, alone_r, join_s, join_r, scal_s, scal_r):
    me = lax.axis_index("sector")
    core = lax.axis_index("op")
    other = 1 - core
    odd = lax.rem(me, 2)
    sign = 1 - 2 * odd
    peer = me + sign
    ahead = lax.rem(me + 2 * sign + n, n)
    behind = lax.rem(me - 2 * sign + n, n)
    terms, nsec = left.shape[0], left.shape[1]
    block = left.shape[2]
    rows = block // n_op
    groups = terms // GROUP
    everyone = n * n_op
    flat = me * n_op + core

    def loads(s, g):
        part = pl.ds(g * GROUP, GROUP)
        return (
            pltpu.make_async_copy(left.at[part, s], lbuf.at[s, part], lsem.at[s, g]),
            pltpu.make_async_copy(right.at[part, s], rbuf.at[s, part], rsem.at[s, g]),
        )

    for s in range(nsec):
        for g in range(groups):
            for copy in loads(s, g):
                copy.start()

    barrier = pltpu.get_barrier_semaphore()

    def greet(i, carry):
        dev = lax.rem(flat + i, everyone)
        pl.semaphore_signal(barrier, inc=1, device_id={"sector": dev // n_op, "op": lax.rem(dev, n_op)},
                            device_id_type=MESH)
        return carry

    lax.fori_loop(1, everyone, greet, 0)

    role_class = (0, 1 + odd, 2 - odd, 3 + odd, 4 - odd)

    def remote(src, dst, send, recv, where):
        return pltpu.make_async_remote_copy(src_ref=src, dst_ref=dst, send_sem=send, recv_sem=recv,
                                            device_id=where, device_id_type=MESH)

    def sib_copy(s):
        return remote(acc.at[s, other], sib.at[s], sib_s.at[s], sib_r.at[s], {"op": other})

    def via_copy(s):
        return remote(tot.at[s, VIA_PEER], via_in.at[s], via_s.at[s], via_r.at[s], {"sector": peer})

    def peer_copy(s):
        return remote(tot.at[s, TO_PEER], peer_in.at[s], peer_s.at[s], peer_r.at[s], {"sector": peer})

    def alone_copy(s):
        return remote(tot.at[s, ALONE], alone_in.at[s], alone_s.at[s], alone_r.at[s], {"sector": behind})

    def joined_copy(s):
        return remote(joined.at[s], joined_in.at[s], join_s.at[s], join_r.at[s], {"sector": ahead})

    def compute(s):
        acc[s] = jnp.zeros(acc.shape[1:], jnp.float32)

        def step(g, carry):
            for copy in loads(s, g):
                copy.wait()
            lhs = lbuf[s, pl.ds(g * GROUP, GROUP)].reshape(GROUP * block, block)
            half = jnp.dot(lhs, w_ref[s], preferred_element_type=jnp.float32).astype(jnp.bfloat16)
            products = [
                lax.dot_general(half[i * block:(i + 1) * block], rbuf[s, g * GROUP + i],
                                (((1,), (1,)), ((), ())), preferred_element_type=jnp.float32)
                for i in range(GROUP)
            ]
            for h in range(n_op):
                for r in range(5):
                    total = acc[s, h, r]
                    for i in range(GROUP):
                        chosen = jnp.where(tc[g * GROUP + i] == role_class[r], 1.0, 0.0)
                        total = total + chosen * products[i][h * rows:(h + 1) * rows]
                    acc[s, h, r] = total
            return carry

        lax.fori_loop(0, groups, step, 0)

    def finish(s):
        sib_copy(s).wait_recv()
        for r in (VIA_PEER, ALONE, TO_PEER, JOINED, OWN):
            tot[s, r] = acc[s, core, r] + sib[s, r]
            if r == VIA_PEER:
                via_copy(s).start()
            if r == ALONE:
                alone_copy(s).start()

    for s in range(nsec):
        compute(s)
        if s == 0:
            pl.semaphore_wait(barrier, everyone - 1)
        sib_copy(s).start()
        if s > 0:
            finish(s - 1)
    finish(nsec - 1)
    for s in range(nsec):
        peer_copy(s).start()

    def weights(source, class_id, dest):
        return [
            [jnp.where(ts[source * nsec + j, class_id] == dest * nsec + t, 1.0, 0.0) for j in range(nsec)]
            for t in range(nsec)
        ]

    own_w = weights(me, 3 + odd, ahead)
    via_w = weights(peer, 1 + odd, ahead)
    for s in range(nsec):
        via_copy(s).wait_recv()
    for t in range(nsec):
        total = own_w[t][0] * tot[0, JOINED] + via_w[t][0] * via_in[0]
        for j in range(1, nsec):
            total = total + own_w[t][j] * tot[j, JOINED] + via_w[t][j] * via_in[j]
        joined[t] = total
        joined_copy(t).start()

    mine = pl.ds(pl.multiple_of(core * rows, rows), rows)
    norm = jnp.zeros((8, 128), jnp.float32)
    proj = jnp.zeros((8, 128), jnp.float32)

    def fold(x):
        y = x.reshape(rows // 8, 8, block).sum(axis=0)
        z = y[:, 0:128]
        for c in range(1, block // 128):
            z = z + y[:, c * 128:(c + 1) * 128]
        return z

    for t in range(nsec):
        amp = w_ref[t, mine, :].astype(jnp.float32)
        norm = norm + fold(amp * amp)
        sig[t] = energy[t] * amp + tot[t, OWN]
    alone_w = weights(ahead, 4 - odd, me)
    for s in range(nsec):
        alone_copy(s).wait_recv()
    for t in range(nsec):
        total = sig[t]
        for j in range(nsec):
            total = total + alone_w[t][j] * alone_in[j]
        sig[t] = total
    peer_w = weights(peer, 2 - odd, me)
    for s in range(nsec):
        peer_copy(s).wait_recv()
    for t in range(nsec):
        total = sig[t]
        for j in range(nsec):
            total = total + peer_w[t][j] * peer_in[j]
        sig[t] = total
    for t in range(nsec):
        joined_copy(t).wait_recv()
        total = sig[t] + joined_in[t]
        sig[t] = total
        proj = proj + fold(w_ref[t, mine, :].astype(jnp.float32) * total)
    scal[0, 0] = proj
    scal[0, 1] = norm

    def scal_copy(i):
        dev = lax.rem(flat + i, everyone)
        return remote(scal.at[0], scal.at[i], scal_s.at[i], scal_r.at[i],
                      {"sector": dev // n_op, "op": lax.rem(dev, n_op)})

    def scal_start(i, carry):
        scal_copy(i).start()
        return carry

    def scal_recv(i, carry):
        scal_copy(i).wait_recv()
        return carry

    def scal_sent(i, carry):
        scal_copy(i).wait_send()
        return carry

    lax.fori_loop(1, everyone, scal_start, 0)
    for t in range(nsec):
        sigma_out[t] = sig[t].astype(jnp.bfloat16)
        sib_copy(t).wait_send()
        via_copy(t).wait_send()
        peer_copy(t).wait_send()
        alone_copy(t).wait_send()
        joined_copy(t).wait_send()
    lax.fori_loop(1, everyone, scal_recv, 0)
    sums = scal[...].sum(axis=0)
    theta = jnp.sum(sums[0], keepdims=True) / jnp.sum(sums[1], keepdims=True)
    for t in range(nsec):
        resid_out[t] = (sig[t] - theta * w_ref[t, mine, :].astype(jnp.float32)).astype(jnp.bfloat16)
    lax.fori_loop(1, everyone, scal_sent, 0)


def local(n, n_op, wavefunction, left_ops, right_ops, energy, term_class, target_sector):
    terms, nsec, block, _ = left_ops.shape
    rows = block // n_op
    vmem = pl.BlockSpec(memory_space=pltpu.VMEM)
    smem = pl.BlockSpec(memory_space=pltpu.SMEM)
    hbm = pl.BlockSpec(memory_space=pl.ANY)
    out = jax.ShapeDtypeStruct((nsec, rows, block), jnp.bfloat16)
    f32 = jnp.float32
    piece = (nsec, rows, block)
    pairs = []
    for _ in range(5):
        pairs += [pltpu.SemaphoreType.DMA((nsec,)), pltpu.SemaphoreType.DMA((nsec,))]
    return pl.pallas_call(
        functools.partial(kernel, n, n_op),
        out_shape=(out, out),
        in_specs=[smem, smem, smem, vmem, hbm, hbm],
        out_specs=(vmem, vmem),
        scratch_shapes=[
            pltpu.VMEM((nsec, terms, block, block), jnp.bfloat16),
            pltpu.VMEM((nsec, terms, block, block), jnp.bfloat16),
            pltpu.VMEM((nsec, n_op, 5, rows, block), f32),
            pltpu.VMEM((nsec, 5, rows, block), f32),
            pltpu.VMEM((nsec, 5, rows, block), f32),
            pltpu.VMEM(piece, f32),
            pltpu.VMEM(piece, f32),
            pltpu.VMEM(piece, f32),
            pltpu.VMEM(piece, f32),
            pltpu.VMEM(piece, f32),
            pltpu.VMEM(piece, f32),
            pltpu.VMEM((n * n_op, 2, 8, 128), f32),
            pltpu.SemaphoreType.DMA((nsec, terms // GROUP)),
            pltpu.SemaphoreType.DMA((nsec, terms // GROUP)),
            *pairs,
            pltpu.SemaphoreType.DMA((n * n_op,)),
            pltpu.SemaphoreType.DMA((n * n_op,)),
        ],
        compiler_params=pltpu.CompilerParams(
            collective_id=0, has_side_effects=True, vmem_limit_bytes=48 * 1024 * 1024
        ),
        cost_estimate=pl.CostEstimate(
            flops=4 * terms * nsec * block**3, bytes_accessed=4 * terms * nsec * block**2, transcendentals=0
        ),
    )(term_class, target_sector, energy, wavefunction, left_ops, right_ops)


def solution(mesh):
    in_specs = (
        P(("groups", "sector"), None, None),
        P("op", ("groups", "sector"), None, None),
        P("op", ("groups", "sector"), None, None),
        P(("groups", "sector")),
        P("op"),
        P("groups", None),
    )
    out_specs = (P(("groups", "sector"), "op", None), P(("groups", "sector"), "op", None))
    body = functools.partial(local, mesh.shape["sector"], mesh.shape["op"])
    return jax.shard_map(body, mesh=mesh, in_specs=in_specs, out_specs=out_specs, check_vma=False)
```

```python
import functools

import jax
import jax.numpy as jnp
from jax import lax
from jax.experimental import pallas as pl
from jax.experimental.pallas import tpu as pltpu
from jax.sharding import PartitionSpec as P

MESH = pl.DeviceIdType.MESH
GROUP = 4
ALONE, VIA_PEER, TO_PEER, JOINED, OWN = range(5)
FIRST = 2
PARTS = 2


def kernel(n, n_op, tc_in, ts_in, energy_in, w_in, left, right, sigma_out, resid_out,
           tc, ts, energy, w_ref, lbuf, rbuf, acc, sib, tot, peer_in, via_in, alone_in, joined_in, joined, sig, scal,
           small, lsem, rsem, sib_s, sib_r, peer_s, peer_r, via_s, via_r, alone_s, alone_r, join_s, join_r, scal_s, scal_r):
    me = lax.axis_index("sector")
    core = lax.axis_index("op")
    other = 1 - core
    odd = lax.rem(me, 2)
    sign = 1 - 2 * odd
    peer = me + sign
    ahead = lax.rem(me + 2 * sign + n, n)
    behind = lax.rem(me - 2 * sign + n, n)
    terms, nsec = left.shape[0], left.shape[1]
    block = left.shape[2]
    rows = block // n_op
    groups = terms // GROUP
    everyone = n * n_op
    flat = me * n_op + core

    def loads(s, g):
        part = pl.ds(g * GROUP, GROUP)
        return (
            pltpu.make_async_copy(left.at[part, s], lbuf.at[s, part], lsem.at[s, g]),
            pltpu.make_async_copy(right.at[part, s], rbuf.at[s, part], rsem.at[s, g]),
        )

    smalls = [
        pltpu.make_async_copy(src, dst, small.at[i])
        for i, (src, dst) in enumerate(((w_in, w_ref), (tc_in, tc), (ts_in, ts), (energy_in, energy)))
    ]
    for copy in smalls:
        copy.start()
    for s in range(nsec):
        for g in range(groups):
            for copy in loads(s, g):
                copy.start()

    barrier = pltpu.get_barrier_semaphore()

    def greet(i, carry):
        dev = lax.rem(flat + i, everyone)
        pl.semaphore_signal(barrier, inc=1, device_id={"sector": dev // n_op, "op": lax.rem(dev, n_op)},
                            device_id_type=MESH)
        return carry

    lax.fori_loop(1, everyone, greet, 0)

    role_class = (4 - odd, 2 - odd, 1 + odd, 3 + odd, 0)

    def remote(src, dst, send, recv, where):
        return pltpu.make_async_remote_copy(src_ref=src, dst_ref=dst, send_sem=send, recv_sem=recv,
                                            device_id=where, device_id_type=MESH)

    part_rows = rows // PARTS

    def sib_copy(s, b):
        roles = pl.ds(0, FIRST) if b == 0 else pl.ds(FIRST, 5 - FIRST)
        return remote(acc.at[s, other, roles], sib.at[s, roles], sib_s.at[s, b], sib_r.at[s, b], {"op": other})

    def via_copy(s, p):
        part = pl.ds(p * part_rows, part_rows)
        return remote(tot.at[s, VIA_PEER, part], via_in.at[s, part], via_s.at[s, p], via_r.at[s, p], {"sector": peer})

    def peer_copy(s):
        return remote(tot.at[s, TO_PEER], peer_in.at[s], peer_s.at[s], peer_r.at[s], {"sector": peer})

    def alone_copy(s):
        return remote(tot.at[s, ALONE], alone_in.at[s], alone_s.at[s], alone_r.at[s], {"sector": behind})

    def joined_copy(s, p):
        part = pl.ds(p * part_rows, part_rows)
        return remote(joined.at[s, part], joined_in.at[s, part], join_s.at[s, p], join_r.at[s, p], {"sector": ahead})

    def compute(s, g):
        for copy in loads(s, g):
            copy.wait()
        lhs = lbuf[s, pl.ds(g * GROUP, GROUP)].reshape(GROUP * block, block)
        half = jnp.dot(lhs, w_ref[s], preferred_element_type=jnp.float32).astype(jnp.bfloat16)
        products = [
            lax.dot_general(half[i * block:(i + 1) * block], rbuf[s, g * GROUP + i],
                            (((1,), (1,)), ((), ())), preferred_element_type=jnp.float32)
            for i in range(GROUP)
        ]
        chosen = [[jnp.where(tc[g * GROUP + i] == c, 1.0, 0.0) for i in range(GROUP)] for c in role_class]
        for h in range(n_op):
            for r in range(5):
                total = chosen[r][0] * products[0][h * rows:(h + 1) * rows]
                for i in range(1, GROUP):
                    total = total + chosen[r][i] * products[i][h * rows:(h + 1) * rows]
                acc[s, h, r] = total if g == 0 else acc[s, h, r] + total

    def finish_first(s):
        sib_copy(s, 0).wait_recv()
        tot[s, ALONE] = acc[s, core, ALONE] + sib[s, ALONE]
        alone_copy(s).start()
        tot[s, VIA_PEER] = acc[s, core, VIA_PEER] + sib[s, VIA_PEER]
        via_copy(s, 0).start()
        if s == 0:
            via_copy(s, 1).start()
        if s == nsec - 1:
            for q in range(1, nsec):
                via_copy(q, 1).start()

    def finish_second(s):
        sib_copy(s, 1).wait_recv()
        for r in (TO_PEER, JOINED, OWN):
            tot[s, r] = acc[s, core, r] + sib[s, r]
        if s == nsec - 1:
            for q in range(nsec):
                peer_copy(q).start()

    for copy in smalls:
        copy.wait()
    for s in range(nsec):
        for g in range(groups):
            compute(s, g)
            if s > 0 and g == 0:
                finish_first(s - 1)
            if s > 0 and g == groups - 1:
                finish_second(s - 1)
        if s == 0:
            pl.semaphore_wait(barrier, everyone - 1)
        for b in range(2):
            sib_copy(s, b).start()
    finish_first(nsec - 1)
    finish_second(nsec - 1)

    def weights(source, class_id, dest):
        return [
            [jnp.where(ts[class_id, source * nsec + j] == dest * nsec + t, 1.0, 0.0) for j in range(nsec)]
            for t in range(nsec)
        ]

    own_w = weights(me, 3 + odd, ahead)
    via_w = weights(peer, 1 + odd, ahead)
    for p in range(PARTS):
        part = pl.ds(p * part_rows, part_rows)
        for s in range(nsec):
            via_copy(s, p).wait_recv()
        for t in range(nsec):
            total = own_w[t][0] * tot[0, JOINED, part] + via_w[t][0] * via_in[0, part]
            for j in range(1, nsec):
                total = total + own_w[t][j] * tot[j, JOINED, part] + via_w[t][j] * via_in[j, part]
            joined[t, part] = total
            joined_copy(t, p).start()

    mine = pl.ds(pl.multiple_of(core * rows, rows), rows)
    norm = jnp.zeros((8, block), jnp.float32)
    proj = jnp.zeros((8, block), jnp.float32)

    def fold(x):
        return x.reshape(x.shape[0] // 8, 8, block).sum(axis=0)

    def narrow(x):
        y = jnp.sum(x, axis=0, keepdims=True)
        z = y[:, 0:128]
        for c in range(1, block // 128):
            z = z + y[:, c * 128:(c + 1) * 128]
        return z

    for t in range(nsec):
        amp = w_ref[t, mine, :].astype(jnp.float32)
        norm = norm + fold(amp * amp)
        sig[t] = energy[t] * amp + tot[t, OWN]
    scal[0, 1:2] = narrow(norm)
    alone_w = weights(ahead, 4 - odd, me)
    for s in range(nsec):
        alone_copy(s).wait_recv()
    for t in range(nsec):
        total = sig[t]
        for j in range(nsec):
            total = total + alone_w[t][j] * alone_in[j]
        sig[t] = total
    peer_w = weights(peer, 2 - odd, me)
    for s in range(nsec):
        peer_copy(s).wait_recv()
    for t in range(nsec):
        total = sig[t]
        for j in range(nsec):
            total = total + peer_w[t][j] * peer_in[j]
        sig[t] = total
    for p in range(PARTS):
        part = pl.ds(p * part_rows, part_rows)
        here = pl.ds(pl.multiple_of(core * rows + p * part_rows, part_rows), part_rows)
        for t in range(nsec):
            joined_copy(t, p).wait_recv()
            total = sig[t, part] + joined_in[t, part]
            sig[t, part] = total
            proj = proj + fold(w_ref[t, here, :].astype(jnp.float32) * total)
    scal[0, 0:1] = narrow(proj)

    def scal_copy(i):
        dev = lax.rem(flat + i, everyone)
        return remote(scal.at[0], scal.at[i], scal_s.at[i], scal_r.at[i],
                      {"sector": dev // n_op, "op": lax.rem(dev, n_op)})

    def scal_start(i, carry):
        scal_copy(i).start()
        return carry

    def scal_recv(i, carry):
        scal_copy(i).wait_recv()
        return carry

    def scal_sent(i, carry):
        scal_copy(i).wait_send()
        return carry

    lax.fori_loop(1, everyone, scal_start, 0)
    for t in range(nsec):
        sigma_out[t] = sig[t].astype(jnp.bfloat16)
        for p in range(2):
            sib_copy(t, p).wait_send()
        for p in range(PARTS):
            via_copy(t, p).wait_send()
            joined_copy(t, p).wait_send()
        peer_copy(t).wait_send()
        alone_copy(t).wait_send()
    lax.fori_loop(1, everyone, scal_recv, 0)
    sums = scal[...].sum(axis=0)
    theta = jnp.sum(sums[0:1], keepdims=True) / jnp.sum(sums[1:2], keepdims=True)
    for t in range(nsec):
        resid_out[t] = (sig[t] - theta * w_ref[t, mine, :].astype(jnp.float32)).astype(jnp.bfloat16)
    lax.fori_loop(1, everyone, scal_sent, 0)


def local(n, n_op, wavefunction, left_ops, right_ops, energy, term_class, target_sector):
    terms, nsec, block, _ = left_ops.shape
    target_sector = target_sector.T
    rows = block // n_op
    vmem = pl.BlockSpec(memory_space=pltpu.VMEM)
    hbm = pl.BlockSpec(memory_space=pl.ANY)
    out = jax.ShapeDtypeStruct((nsec, rows, block), jnp.bfloat16)
    f32 = jnp.float32
    piece = (nsec, rows, block)
    pairs = []
    for count in ((nsec, 2), (nsec,), (nsec, PARTS), (nsec,), (nsec, PARTS)):
        pairs += [pltpu.SemaphoreType.DMA(count), pltpu.SemaphoreType.DMA(count)]
    return pl.pallas_call(
        functools.partial(kernel, n, n_op),
        out_shape=(out, out),
        in_specs=[hbm] * 6,
        out_specs=(vmem, vmem),
        scratch_shapes=[
            pltpu.SMEM((terms,), jnp.int32),
            pltpu.SMEM(target_sector.shape, jnp.int32),
            pltpu.SMEM((nsec,), f32),
            pltpu.VMEM((nsec, block, block), jnp.bfloat16),
            pltpu.VMEM((nsec, terms, block, block), jnp.bfloat16),
            pltpu.VMEM((nsec, terms, block, block), jnp.bfloat16),
            pltpu.VMEM((nsec, n_op, 5, rows, block), f32),
            pltpu.VMEM((nsec, 5, rows, block), f32),
            pltpu.VMEM((nsec, 5, rows, block), f32),
            pltpu.VMEM(piece, f32),
            pltpu.VMEM(piece, f32),
            pltpu.VMEM(piece, f32),
            pltpu.VMEM(piece, f32),
            pltpu.VMEM(piece, f32),
            pltpu.VMEM(piece, f32),
            pltpu.VMEM((n * n_op, 2, 128), f32),
            pltpu.SemaphoreType.DMA((4,)),
            pltpu.SemaphoreType.DMA((nsec, terms // GROUP)),
            pltpu.SemaphoreType.DMA((nsec, terms // GROUP)),
            *pairs,
            pltpu.SemaphoreType.DMA((n * n_op,)),
            pltpu.SemaphoreType.DMA((n * n_op,)),
        ],
        compiler_params=pltpu.CompilerParams(
            collective_id=0, has_side_effects=True, vmem_limit_bytes=60 * 1024 * 1024
        ),
        cost_estimate=pl.CostEstimate(
            flops=4 * terms * nsec * block**3, bytes_accessed=4 * terms * nsec * block**2, transcendentals=0
        ),
    )(term_class, target_sector, energy, wavefunction, left_ops, right_ops)


def solution(mesh):
    in_specs = (
        P(("groups", "sector"), None, None),
        P("op", ("groups", "sector"), None, None),
        P("op", ("groups", "sector"), None, None),
        P(("groups", "sector")),
        P("op"),
        P("groups", None),
    )
    out_specs = (P(("groups", "sector"), "op", None), P(("groups", "sector"), "op", None))
    body = functools.partial(local, mesh.shape["sector"], mesh.shape["op"])
    return jax.shard_map(body, mesh=mesh, in_specs=in_specs, out_specs=out_specs, check_vma=False)
```

```python
import functools

import jax
import jax.numpy as jnp
from jax import lax
from jax.experimental import pallas as pl
from jax.experimental.pallas import tpu as pltpu
from jax.sharding import PartitionSpec as P

MESH = pl.DeviceIdType.MESH
GROUP = 8
ALONE, VIA_PEER, TO_PEER, JOINED, OWN = range(5)
FIRST = 2
PARTS = 2


def kernel(n, n_op, tc_in, ts_in, energy_in, w_in, left, right, sigma_out, resid_out,
           tc, ts, energy, w_ref, lbuf, rbuf, acc, sib, tot, peer_in, via_in, alone_in, joined_in, joined, sig, scal,
           small, lsem, rsem, sib_s, sib_r, peer_s, peer_r, via_s, via_r, alone_s, alone_r, join_s, join_r, scal_s, scal_r):
    me = lax.axis_index("sector")
    core = lax.axis_index("op")
    other = 1 - core
    odd = lax.rem(me, 2)
    sign = 1 - 2 * odd
    peer = me + sign
    ahead = lax.rem(me + 2 * sign + n, n)
    behind = lax.rem(me - 2 * sign + n, n)
    terms, nsec = left.shape[0], left.shape[1]
    block = left.shape[2]
    rows = block // n_op
    groups = terms // GROUP
    everyone = n * n_op
    flat = me * n_op + core

    def loads(s, g):
        part = pl.ds(g * GROUP, GROUP)
        return (
            pltpu.make_async_copy(left.at[part, s], lbuf.at[s, part], lsem.at[s, g]),
            pltpu.make_async_copy(right.at[part, s], rbuf.at[s, part], rsem.at[s, g]),
        )

    smalls = [
        pltpu.make_async_copy(src, dst, small.at[i])
        for i, (src, dst) in enumerate(((w_in, w_ref), (tc_in, tc), (ts_in, ts), (energy_in, energy)))
    ]
    for copy in smalls:
        copy.start()
    for s in range(nsec):
        for g in range(groups):
            for copy in loads(s, g):
                copy.start()

    barrier = pltpu.get_barrier_semaphore()

    def greet(i, carry):
        dev = lax.rem(flat + i, everyone)
        pl.semaphore_signal(barrier, inc=1, device_id={"sector": dev // n_op, "op": lax.rem(dev, n_op)},
                            device_id_type=MESH)
        return carry

    lax.fori_loop(1, everyone, greet, 0)

    role_class = (4 - odd, 2 - odd, 1 + odd, 3 + odd, 0)

    def remote(src, dst, send, recv, where):
        return pltpu.make_async_remote_copy(src_ref=src, dst_ref=dst, send_sem=send, recv_sem=recv,
                                            device_id=where, device_id_type=MESH)

    part_rows = rows // PARTS

    def sib_copy(s, b):
        roles = pl.ds(0, FIRST) if b == 0 else pl.ds(FIRST, 5 - FIRST)
        return remote(acc.at[s, other, roles], sib.at[s, roles], sib_s.at[s, b], sib_r.at[s, b], {"op": other})

    def via_copy(s, p):
        part = pl.ds(p * part_rows, part_rows)
        return remote(tot.at[s, VIA_PEER, part], via_in.at[s, part], via_s.at[s, p], via_r.at[s, p], {"sector": peer})

    def peer_copy(s):
        return remote(tot.at[s, TO_PEER], peer_in.at[s], peer_s.at[s], peer_r.at[s], {"sector": peer})

    def alone_copy(s):
        return remote(tot.at[s, ALONE], alone_in.at[s], alone_s.at[s], alone_r.at[s], {"sector": behind})

    def joined_copy(s, p):
        part = pl.ds(p * part_rows, part_rows)
        return remote(joined.at[s, part], joined_in.at[s, part], join_s.at[s, p], join_r.at[s, p], {"sector": ahead})

    def compute(s, g):
        for copy in loads(s, g):
            copy.wait()
        lhs = lbuf[s, pl.ds(g * GROUP, GROUP)].reshape(GROUP * block, block)
        half = jnp.dot(lhs, w_ref[s], preferred_element_type=jnp.float32).astype(jnp.bfloat16)
        products = [
            lax.dot_general(half[i * block:(i + 1) * block], rbuf[s, g * GROUP + i],
                            (((1,), (1,)), ((), ())), preferred_element_type=jnp.float32)
            for i in range(GROUP)
        ]
        chosen = [[jnp.where(tc[g * GROUP + i] == c, 1.0, 0.0) for i in range(GROUP)] for c in role_class]
        for h in range(n_op):
            for r in range(5):
                total = chosen[r][0] * products[0][h * rows:(h + 1) * rows]
                for i in range(1, GROUP):
                    total = total + chosen[r][i] * products[i][h * rows:(h + 1) * rows]
                acc[s, h, r] = acc[s, h, r] + total

    def finish_first(s):
        sib_copy(s, 0).wait_recv()
        tot[s, ALONE] = acc[s, core, ALONE] + sib[s, ALONE]
        alone_copy(s).start()
        tot[s, VIA_PEER] = acc[s, core, VIA_PEER] + sib[s, VIA_PEER]
        via_copy(s, 0).start()
        if s == 0:
            via_copy(s, 1).start()
        if s == nsec - 1:
            for q in range(1, nsec):
                via_copy(q, 1).start()

    def finish_second(s):
        sib_copy(s, 1).wait_recv()
        for r in (TO_PEER, JOINED, OWN):
            tot[s, r] = acc[s, core, r] + sib[s, r]
        if s == nsec - 1:
            for q in range(nsec):
                peer_copy(q).start()

    for copy in smalls:
        copy.wait()
    for s in range(nsec):
        acc[s] = jnp.zeros(acc.shape[1:], jnp.float32)
        middle = groups // 2 if s > 0 else 0

        def step(g, carry, s=s):
            compute(s, g)
            return carry

        lax.fori_loop(0, middle, step, 0)
        if s > 0:
            finish_first(s - 1)
        lax.fori_loop(middle, groups, step, 0)
        if s > 0:
            finish_second(s - 1)
        if s == 0:
            pl.semaphore_wait(barrier, everyone - 1)
        for b in range(2):
            sib_copy(s, b).start()
    finish_first(nsec - 1)
    finish_second(nsec - 1)

    def weights(source, class_id, dest):
        return [
            [jnp.where(ts[class_id, source * nsec + j] == dest * nsec + t, 1.0, 0.0) for j in range(nsec)]
            for t in range(nsec)
        ]

    own_w = weights(me, 3 + odd, ahead)
    via_w = weights(peer, 1 + odd, ahead)
    for p in range(PARTS):
        part = pl.ds(p * part_rows, part_rows)
        for s in range(nsec):
            via_copy(s, p).wait_recv()
        for t in range(nsec):
            total = own_w[t][0] * tot[0, JOINED, part] + via_w[t][0] * via_in[0, part]
            for j in range(1, nsec):
                total = total + own_w[t][j] * tot[j, JOINED, part] + via_w[t][j] * via_in[j, part]
            joined[t, part] = total
            joined_copy(t, p).start()

    mine = pl.ds(pl.multiple_of(core * rows, rows), rows)
    norm = jnp.zeros((8, block), jnp.float32)
    proj = jnp.zeros((8, block), jnp.float32)

    def fold(x):
        return x.reshape(x.shape[0] // 8, 8, block).sum(axis=0)

    def narrow(x):
        y = jnp.sum(x, axis=0, keepdims=True)
        z = y[:, 0:128]
        for c in range(1, block // 128):
            z = z + y[:, c * 128:(c + 1) * 128]
        return z

    for t in range(nsec):
        amp = w_ref[t, mine, :].astype(jnp.float32)
        norm = norm + fold(amp * amp)
        sig[t] = energy[t] * amp + tot[t, OWN]
    scal[0, 1:2] = narrow(norm)
    alone_w = weights(ahead, 4 - odd, me)
    for s in range(nsec):
        alone_copy(s).wait_recv()
    for t in range(nsec):
        total = sig[t]
        for j in range(nsec):
            total = total + alone_w[t][j] * alone_in[j]
        sig[t] = total
    peer_w = weights(peer, 2 - odd, me)
    for s in range(nsec):
        peer_copy(s).wait_recv()
    for t in range(nsec):
        total = sig[t]
        for j in range(nsec):
            total = total + peer_w[t][j] * peer_in[j]
        sig[t] = total
    for p in range(PARTS):
        part = pl.ds(p * part_rows, part_rows)
        here = pl.ds(pl.multiple_of(core * rows + p * part_rows, part_rows), part_rows)
        for t in range(nsec):
            joined_copy(t, p).wait_recv()
            total = sig[t, part] + joined_in[t, part]
            sig[t, part] = total
            proj = proj + fold(w_ref[t, here, :].astype(jnp.float32) * total)
    scal[0, 0:1] = narrow(proj)

    def scal_copy(i):
        dev = lax.rem(flat + i, everyone)
        return remote(scal.at[0], scal.at[i], scal_s.at[i], scal_r.at[i],
                      {"sector": dev // n_op, "op": lax.rem(dev, n_op)})

    def scal_start(i, carry):
        scal_copy(i).start()
        return carry

    def scal_recv(i, carry):
        scal_copy(i).wait_recv()
        return carry

    def scal_sent(i, carry):
        scal_copy(i).wait_send()
        return carry

    lax.fori_loop(1, everyone, scal_start, 0)
    for t in range(nsec):
        sigma_out[t] = sig[t].astype(jnp.bfloat16)
        for p in range(2):
            sib_copy(t, p).wait_send()
        for p in range(PARTS):
            via_copy(t, p).wait_send()
            joined_copy(t, p).wait_send()
        peer_copy(t).wait_send()
        alone_copy(t).wait_send()
    lax.fori_loop(1, everyone, scal_recv, 0)
    sums = scal[...].sum(axis=0)
    theta = jnp.sum(sums[0:1], keepdims=True) / jnp.sum(sums[1:2], keepdims=True)
    for t in range(nsec):
        resid_out[t] = (sig[t] - theta * w_ref[t, mine, :].astype(jnp.float32)).astype(jnp.bfloat16)
    lax.fori_loop(1, everyone, scal_sent, 0)


def local(n, n_op, wavefunction, left_ops, right_ops, energy, term_class, target_sector):
    terms, nsec, block, _ = left_ops.shape
    target_sector = target_sector.T
    rows = block // n_op
    vmem = pl.BlockSpec(memory_space=pltpu.VMEM)
    hbm = pl.BlockSpec(memory_space=pl.ANY)
    out = jax.ShapeDtypeStruct((nsec, rows, block), jnp.bfloat16)
    f32 = jnp.float32
    piece = (nsec, rows, block)
    pairs = []
    for count in ((nsec, 2), (nsec,), (nsec, PARTS), (nsec,), (nsec, PARTS)):
        pairs += [pltpu.SemaphoreType.DMA(count), pltpu.SemaphoreType.DMA(count)]
    return pl.pallas_call(
        functools.partial(kernel, n, n_op),
        out_shape=(out, out),
        in_specs=[hbm] * 6,
        out_specs=(vmem, vmem),
        scratch_shapes=[
            pltpu.SMEM((terms,), jnp.int32),
            pltpu.SMEM(target_sector.shape, jnp.int32),
            pltpu.SMEM((nsec,), f32),
            pltpu.VMEM((nsec, block, block), jnp.bfloat16),
            pltpu.VMEM((nsec, terms, block, block), jnp.bfloat16),
            pltpu.VMEM((nsec, terms, block, block), jnp.bfloat16),
            pltpu.VMEM((nsec, n_op, 5, rows, block), f32),
            pltpu.VMEM((nsec, 5, rows, block), f32),
            pltpu.VMEM((nsec, 5, rows, block), f32),
            pltpu.VMEM(piece, f32),
            pltpu.VMEM(piece, f32),
            pltpu.VMEM(piece, f32),
            pltpu.VMEM(piece, f32),
            pltpu.VMEM(piece, f32),
            pltpu.VMEM(piece, f32),
            pltpu.VMEM((n * n_op, 2, 128), f32),
            pltpu.SemaphoreType.DMA((4,)),
            pltpu.SemaphoreType.DMA((nsec, terms // GROUP)),
            pltpu.SemaphoreType.DMA((nsec, terms // GROUP)),
            *pairs,
            pltpu.SemaphoreType.DMA((n * n_op,)),
            pltpu.SemaphoreType.DMA((n * n_op,)),
        ],
        compiler_params=pltpu.CompilerParams(
            collective_id=0, has_side_effects=True, vmem_limit_bytes=60 * 1024 * 1024
        ),
        cost_estimate=pl.CostEstimate(
            flops=4 * terms * nsec * block**3, bytes_accessed=4 * terms * nsec * block**2, transcendentals=0
        ),
    )(term_class, target_sector, energy, wavefunction, left_ops, right_ops)


def solution(mesh):
    in_specs = (
        P(("groups", "sector"), None, None),
        P("op", ("groups", "sector"), None, None),
        P("op", ("groups", "sector"), None, None),
        P(("groups", "sector")),
        P("op"),
        P("groups", None),
    )
    out_specs = (P(("groups", "sector"), "op", None), P(("groups", "sector"), "op", None))
    body = functools.partial(local, mesh.shape["sector"], mesh.shape["op"])
    return jax.shard_map(body, mesh=mesh, in_specs=in_specs, out_specs=out_specs, check_vma=False)
```

```python
import functools

import jax
import jax.numpy as jnp
from jax import lax
from jax.experimental import pallas as pl
from jax.experimental.pallas import tpu as pltpu
from jax.sharding import PartitionSpec as P

MESH = pl.DeviceIdType.MESH
GROUP = 8
ALONE, VIA_PEER, TO_PEER, JOINED, OWN = range(5)
FIRST = 2
PARTS = 2


def kernel(n, n_op, tc_in, ts_in, energy_in, w_in, left, right, sigma_out, resid_out,
           tc, ts, energy, w_ref, lbuf, rbuf, acc, sib, tot, peer_in, via_in, alone_in, joined_in, joined, sig, scal,
           small, lsem, rsem, sib_s, sib_r, peer_s, peer_r, via_s, via_r, alone_s, alone_r, join_s, join_r, scal_s, scal_r):
    me = lax.axis_index("sector")
    core = lax.axis_index("op")
    other = 1 - core
    odd = lax.rem(me, 2)
    sign = 1 - 2 * odd
    peer = me + sign
    ahead = lax.rem(me + 2 * sign + n, n)
    behind = lax.rem(me - 2 * sign + n, n)
    terms, nsec = left.shape[0], left.shape[1]
    block = left.shape[2]
    rows = block // n_op
    groups = terms // GROUP
    everyone = n * n_op
    flat = me * n_op + core

    def loads(s, g):
        part = pl.ds(g * GROUP, GROUP)
        return (
            pltpu.make_async_copy(left.at[part, s], lbuf.at[s, part], lsem.at[s, g]),
            pltpu.make_async_copy(right.at[part, s], rbuf.at[s, part], rsem.at[s, g]),
        )

    smalls = [
        pltpu.make_async_copy(src, dst, small.at[i])
        for i, (src, dst) in enumerate(((w_in, w_ref), (tc_in, tc), (ts_in, ts), (energy_in, energy)))
    ]
    for copy in smalls:
        copy.start()
    for s in range(nsec):
        for g in range(groups):
            for copy in loads(s, g):
                copy.start()

    barrier = pltpu.get_barrier_semaphore()

    def greet(i, carry):
        dev = lax.rem(flat + i, everyone)
        pl.semaphore_signal(barrier, inc=1, device_id={"sector": dev // n_op, "op": lax.rem(dev, n_op)},
                            device_id_type=MESH)
        return carry

    lax.fori_loop(1, everyone, greet, 0)

    role_class = (4 - odd, 2 - odd, 1 + odd, 3 + odd, 0)

    def remote(src, dst, send, recv, where):
        return pltpu.make_async_remote_copy(src_ref=src, dst_ref=dst, send_sem=send, recv_sem=recv,
                                            device_id=where, device_id_type=MESH)

    part_rows = rows // PARTS

    def sib_copy(s, b):
        roles = pl.ds(0, FIRST) if b == 0 else pl.ds(FIRST, 5 - FIRST)
        return remote(acc.at[s, other, roles], sib.at[s, roles], sib_s.at[s, b], sib_r.at[s, b], {"op": other})

    def via_copy(s, p):
        part = pl.ds(p * part_rows, part_rows)
        return remote(tot.at[s, VIA_PEER, part], via_in.at[s, part], via_s.at[s, p], via_r.at[s, p], {"sector": peer})

    def peer_copy(s):
        return remote(tot.at[s, TO_PEER], peer_in.at[s], peer_s.at[s], peer_r.at[s], {"sector": peer})

    def alone_copy(s):
        return remote(tot.at[s, ALONE], alone_in.at[s], alone_s.at[s], alone_r.at[s], {"sector": behind})

    def joined_copy(s, p):
        part = pl.ds(p * part_rows, part_rows)
        return remote(joined.at[s, part], joined_in.at[s, part], join_s.at[s, p], join_r.at[s, p], {"sector": ahead})

    def compute(s, g):
        for copy in loads(s, g):
            copy.wait()
        lhs = lbuf[s, pl.ds(g * GROUP, GROUP)].reshape(GROUP * block, block)
        half = jnp.dot(lhs, w_ref[s], preferred_element_type=jnp.float32).astype(jnp.bfloat16)
        products = [
            lax.dot_general(half[i * block:(i + 1) * block], rbuf[s, g * GROUP + i],
                            (((1,), (1,)), ((), ())), preferred_element_type=jnp.float32)
            for i in range(GROUP)
        ]
        chosen = [[jnp.where(tc[g * GROUP + i] == c, 1.0, 0.0) for i in range(GROUP)] for c in role_class]
        for h in range(n_op):
            for r in range(5):
                total = chosen[r][0] * products[0][h * rows:(h + 1) * rows]
                for i in range(1, GROUP):
                    total = total + chosen[r][i] * products[i][h * rows:(h + 1) * rows]
                acc[s, h, r] = acc[s, h, r] + total

    def finish_first(s):
        sib_copy(s, 0).wait_recv()
        tot[s, ALONE] = acc[s, core, ALONE] + sib[s, ALONE]
        alone_copy(s).start()
        tot[s, VIA_PEER] = acc[s, core, VIA_PEER] + sib[s, VIA_PEER]
        via_copy(s, 0).start()
        if s == 0:
            via_copy(s, 1).start()
        if s == nsec - 1:
            for q in range(1, nsec):
                via_copy(q, 1).start()

    def finish_second(s):
        sib_copy(s, 1).wait_recv()
        for r in (TO_PEER, JOINED, OWN):
            tot[s, r] = acc[s, core, r] + sib[s, r]

    for copy in smalls:
        copy.wait()
    for s in range(nsec):
        acc[s] = jnp.zeros(acc.shape[1:], jnp.float32)
        middle = groups // 2 if s > 0 else 0

        def step(g, carry, s=s):
            compute(s, g)
            return carry

        lax.fori_loop(0, middle, step, 0)
        if s > 0:
            finish_first(s - 1)
        lax.fori_loop(middle, groups, step, 0)
        if s > 0:
            finish_second(s - 1)
        if s == 0:
            pl.semaphore_wait(barrier, everyone - 1)
        for b in range(2):
            sib_copy(s, b).start()
    finish_first(nsec - 1)
    finish_second(nsec - 1)

    def weights(source, class_id, dest):
        return [
            [jnp.where(ts[class_id, source * nsec + j] == dest * nsec + t, 1.0, 0.0) for j in range(nsec)]
            for t in range(nsec)
        ]

    own_w = weights(me, 3 + odd, ahead)
    via_w = weights(peer, 1 + odd, ahead)
    for p in range(PARTS):
        part = pl.ds(p * part_rows, part_rows)
        for s in range(nsec):
            via_copy(s, p).wait_recv()
        for t in range(nsec):
            total = own_w[t][0] * tot[0, JOINED, part] + via_w[t][0] * via_in[0, part]
            for j in range(1, nsec):
                total = total + own_w[t][j] * tot[j, JOINED, part] + via_w[t][j] * via_in[j, part]
            joined[t, part] = total
            joined_copy(t, p).start()
        for q in range(nsec):
            if min(q, PARTS - 1) == p:
                peer_copy(q).start()

    mine = pl.ds(pl.multiple_of(core * rows, rows), rows)
    norm = jnp.zeros((8, block), jnp.float32)
    proj = jnp.zeros((8, block), jnp.float32)

    def fold(x):
        return x.reshape(x.shape[0] // 8, 8, block).sum(axis=0)

    def narrow(x):
        y = jnp.sum(x, axis=0, keepdims=True)
        z = y[:, 0:128]
        for c in range(1, block // 128):
            z = z + y[:, c * 128:(c + 1) * 128]
        return z

    for t in range(nsec):
        amp = w_ref[t, mine, :].astype(jnp.float32)
        norm = norm + fold(amp * amp)
        sig[t] = energy[t] * amp + tot[t, OWN]
    scal[0, 1:2] = narrow(norm)
    alone_w = weights(ahead, 4 - odd, me)
    for s in range(nsec):
        alone_copy(s).wait_recv()
    for t in range(nsec):
        total = sig[t]
        for j in range(nsec):
            total = total + alone_w[t][j] * alone_in[j]
        sig[t] = total
    peer_w = weights(peer, 2 - odd, me)
    for s in range(nsec):
        peer_copy(s).wait_recv()
    for t in range(nsec):
        total = sig[t]
        for j in range(nsec):
            total = total + peer_w[t][j] * peer_in[j]
        sig[t] = total
    for p in range(PARTS):
        part = pl.ds(p * part_rows, part_rows)
        here = pl.ds(pl.multiple_of(core * rows + p * part_rows, part_rows), part_rows)
        for t in range(nsec):
            joined_copy(t, p).wait_recv()
            total = sig[t, part] + joined_in[t, part]
            sig[t, part] = total
            proj = proj + fold(w_ref[t, here, :].astype(jnp.float32) * total)
    scal[0, 0:1] = narrow(proj)

    def scal_copy(i):
        dev = lax.rem(flat + i, everyone)
        return remote(scal.at[0], scal.at[i], scal_s.at[i], scal_r.at[i],
                      {"sector": dev // n_op, "op": lax.rem(dev, n_op)})

    def scal_start(i, carry):
        scal_copy(i).start()
        return carry

    def scal_recv(i, carry):
        scal_copy(i).wait_recv()
        return carry

    def scal_sent(i, carry):
        scal_copy(i).wait_send()
        return carry

    lax.fori_loop(1, everyone, scal_start, 0)
    for t in range(nsec):
        sigma_out[t] = sig[t].astype(jnp.bfloat16)
        for p in range(2):
            sib_copy(t, p).wait_send()
        for p in range(PARTS):
            via_copy(t, p).wait_send()
            joined_copy(t, p).wait_send()
        peer_copy(t).wait_send()
        alone_copy(t).wait_send()
    lax.fori_loop(1, everyone, scal_recv, 0)
    sums = scal[...].sum(axis=0)
    theta = jnp.sum(sums[0:1], keepdims=True) / jnp.sum(sums[1:2], keepdims=True)
    for t in range(nsec):
        resid_out[t] = (sig[t] - theta * w_ref[t, mine, :].astype(jnp.float32)).astype(jnp.bfloat16)
    lax.fori_loop(1, everyone, scal_sent, 0)


def local(n, n_op, wavefunction, left_ops, right_ops, energy, term_class, target_sector):
    terms, nsec, block, _ = left_ops.shape
    target_sector = target_sector.T
    rows = block // n_op
    vmem = pl.BlockSpec(memory_space=pltpu.VMEM)
    hbm = pl.BlockSpec(memory_space=pl.ANY)
    out = jax.ShapeDtypeStruct((nsec, rows, block), jnp.bfloat16)
    f32 = jnp.float32
    piece = (nsec, rows, block)
    pairs = []
    for count in ((nsec, 2), (nsec,), (nsec, PARTS), (nsec,), (nsec, PARTS)):
        pairs += [pltpu.SemaphoreType.DMA(count), pltpu.SemaphoreType.DMA(count)]
    return pl.pallas_call(
        functools.partial(kernel, n, n_op),
        out_shape=(out, out),
        in_specs=[hbm] * 6,
        out_specs=(vmem, vmem),
        scratch_shapes=[
            pltpu.SMEM((terms,), jnp.int32),
            pltpu.SMEM(target_sector.shape, jnp.int32),
            pltpu.SMEM((nsec,), f32),
            pltpu.VMEM((nsec, block, block), jnp.bfloat16),
            pltpu.VMEM((nsec, terms, block, block), jnp.bfloat16),
            pltpu.VMEM((nsec, terms, block, block), jnp.bfloat16),
            pltpu.VMEM((nsec, n_op, 5, rows, block), f32),
            pltpu.VMEM((nsec, 5, rows, block), f32),
            pltpu.VMEM((nsec, 5, rows, block), f32),
            pltpu.VMEM(piece, f32),
            pltpu.VMEM(piece, f32),
            pltpu.VMEM(piece, f32),
            pltpu.VMEM(piece, f32),
            pltpu.VMEM(piece, f32),
            pltpu.VMEM(piece, f32),
            pltpu.VMEM((n * n_op, 2, 128), f32),
            pltpu.SemaphoreType.DMA((4,)),
            pltpu.SemaphoreType.DMA((nsec, terms // GROUP)),
            pltpu.SemaphoreType.DMA((nsec, terms // GROUP)),
            *pairs,
            pltpu.SemaphoreType.DMA((n * n_op,)),
            pltpu.SemaphoreType.DMA((n * n_op,)),
        ],
        compiler_params=pltpu.CompilerParams(
            collective_id=0, has_side_effects=True, vmem_limit_bytes=60 * 1024 * 1024
        ),
        cost_estimate=pl.CostEstimate(
            flops=4 * terms * nsec * block**3, bytes_accessed=4 * terms * nsec * block**2, transcendentals=0
        ),
    )(term_class, target_sector, energy, wavefunction, left_ops, right_ops)


def solution(mesh):
    in_specs = (
        P(("groups", "sector"), None, None),
        P("op", ("groups", "sector"), None, None),
        P("op", ("groups", "sector"), None, None),
        P(("groups", "sector")),
        P("op"),
        P("groups", None),
    )
    out_specs = (P(("groups", "sector"), "op", None), P(("groups", "sector"), "op", None))
    body = functools.partial(local, mesh.shape["sector"], mesh.shape["op"])
    return jax.shard_map(body, mesh=mesh, in_specs=in_specs, out_specs=out_specs, check_vma=False)
```
